512 devices in a mesh: row: 32 (over y, z_lo, core), col: 16 (over x, z_hi).
Axes of the slice: x: 4, y: 8, z: 8 (z_hi: 4, z_lo: 2; z = z_hi * 2 + z_lo), core: 2. Of those that a mesh axis runs over, the one named last changes fastest.
Arguments:
- inputs: bfloat16 [256, 12288], P('col', 'row'), may hold values from -6 to 6
- w_in: bfloat16 [12288, 24576], P('row', 'col'), may hold values from -0.0546875 to 0.0546875
- w_out: bfloat16 [24576, 12288], P('col', 'row'), may hold values from -0.0390625 to 0.0390625
- out_grad: bfloat16 [256, 12288], P('col', 'row'), may hold values from -1.5 to 1.5
Outputs:
- output: bfloat16 [256, 12288], P('col', 'row')
- grad_in: bfloat16 [256, 12288], P('col', 'row')
- grad_w_in: bfloat16 [12288, 24576], P('row', 'col')
- grad_w_out: bfloat16 [24576, 12288], P('col', 'row')
The draws below stay inside these ranges and needn't reach their ends.
All inputs are finite; a program needn't handle non-finite values.
Results may differ from the reference program's by a relative error of at most 0.005.
Values may be sent and summed in bfloat16 or wider, within the bound.
A program may use at most 64 MiB of HBM per device.

```python
import jax
import jax.numpy as jnp

D = 12288
H = 24576
TOKENS = 256


def raised(values, rng, source, target, blocks, factor):
    owner, partner = [(jnp.arange(values.shape[axis_at]) // (values.shape[axis_at] // blocks)).reshape([-1 if axis == axis_at else 1 for axis in range(values.ndim)]) for axis_at in (source, target)]
    chosen = jax.random.permutation(rng, blocks)[partner]
    strong = (owner == chosen) | (owner == (partner + blocks // 2) % blocks)
    return jnp.where(strong, factor * values, values)


def level_of(key, extent, pieces, least, top_value):
    level, own = 1.0, jax.random.fold_in(key, 6)
    for dim, parts in pieces:
        draws = jnp.exp(jax.random.uniform(jax.random.fold_in(own, dim), (parts,), jnp.float32, least / len(pieces), top_value / len(pieces)))
        level = level * jnp.repeat(draws, extent[dim] // parts).reshape([-1 if axis == dim else 1 for axis in range(len(extent))])
    return level


def bell_draw(own_key, extent, deviation, reach, shards=(), dtype=jnp.bfloat16):
    drawn = jax.random.normal(own_key, extent, jnp.float32) * deviation
    if len(shards) > 0:
        drawn = level_of(own_key, extent, shards, -0.22, 0.18) * drawn
    return jnp.clip(drawn, min=-reach, max=reach).astype(dtype)


def noise_with(rng, extent, scale, limit, pieces, heavy, kind=jnp.bfloat16):
    array = scale * jax.random.normal(rng, extent, jnp.float32)
    if pieces:
        array = array * level_of(rng, extent, pieces, -0.22, 0.18)
    return jnp.clip(raised(array, jax.random.fold_in(rng, 3), *heavy), -limit, limit).astype(kind)


def setup_inputs(seed: int = 0) -> dict:
    streams_of = jax.random.split(jax.random.key(seed), 5)
    inputs = noise_with(streams_of[0], (TOKENS, D), 1.0, 6.0, ((0, 16), (1, 32)), (1, 0, 32, 2.75))
    w_in = bell_draw(streams_of[1], (D, H), D ** -0.5, 0.0546875, ((0, 32), (1, 16)))
    w_out = bell_draw(streams_of[2], (H, D), H ** -0.5, 0.0390625, ((0, 16), (1, 32)))
    out_grad = noise_with(streams_of[3], (TOKENS, D), 0.25, 1.5, ((0, 16), (1, 32)), (1, 0, 32, 2.75))
    return {"inputs": inputs, "w_in": w_in, "w_out": w_out, "out_grad": out_grad}


gelu_coef = 0.7978845608028654


def gelu_tanh(value):
    inner = gelu_coef * (value + 0.044715 * value * value * value)
    return 0.5 * value * (1.0 + jnp.tanh(inner))


def gelu_slope(value):
    inner = gelu_coef * (value + 0.044715 * value * value * value)
    tanh_val = jnp.tanh(inner)
    return 0.5 * (1.0 + tanh_val) + 0.5 * value * (1.0 - tanh_val * tanh_val) * gelu_coef * (1.0 + 3.0 * 0.044715 * value * value)


def reference(inputs, w_in, w_out, out_grad):
    pre = jnp.dot(inputs, w_in, preferred_element_type=jnp.float32)
    hidden = gelu_tanh(pre).astype(jnp.bfloat16)
    output = jnp.dot(hidden, w_out, preferred_element_type=jnp.float32).astype(jnp.bfloat16)
    back = jnp.dot(out_grad, w_out.T, preferred_element_type=jnp.float32)
    pre_grad = (back * gelu_slope(pre)).astype(jnp.bfloat16)
    grad_w_out = jnp.dot(hidden.T, out_grad, preferred_element_type=jnp.float32).astype(jnp.bfloat16)
    grad_w_in = jnp.dot(inputs.T, pre_grad, preferred_element_type=jnp.float32).astype(jnp.bfloat16)
    grad_in = jnp.dot(pre_grad, w_in.T, preferred_element_type=jnp.float32).astype(jnp.bfloat16)
    return (output, grad_in, grad_w_in, grad_w_out)
```

```python
import jax
import jax.numpy as jnp
from jax import lax
from jax.experimental import pallas as pl
from jax.experimental.pallas import tpu as pltpu
from jax.sharding import PartitionSpec as P

MESH = pl.DeviceIdType.MESH
BF16, F32 = jnp.bfloat16, jnp.float32
NY, NZL, NK, NX, NZH = 8, 2, 2, 4, 4
TOK, FEAT, HID, HALF = 256, 384, 1536, 768
CHUNK = 16
RING8 = (4, 3, 5, 2, 6, 1, 7)
RING4 = (2, 1, 3)

gelu_coef = 0.7978845608028654


def gelu_and_slope(value):
    inner = gelu_coef * (value + 0.044715 * value * value * value)
    tanh_val = jnp.tanh(inner)
    gelu = 0.5 * value * (1.0 + tanh_val)
    slope = 0.5 * (1.0 + tanh_val) + 0.5 * value * (1.0 - tanh_val * tanh_val) * gelu_coef * (
        1.0 + 3.0 * 0.044715 * value * value
    )
    return gelu, slope


def dot_nn(a, b):
    return lax.dot_general(a, b, (((1,), (0,)), ((), ())), preferred_element_type=F32)


def dot_nt(a, b):
    return lax.dot_general(a, b, (((1,), (1,)), ((), ())), preferred_element_type=F32)


def dot_tn(a, b):
    return lax.dot_general(a, b, (((0,), (0,)), ((), ())), preferred_element_type=F32)


def rows(index, size):
    return pl.ds(pl.multiple_of(index * size, size), size)


def kernel(
    inp_hbm, og_hbm, win_hbm, wout_hbm,
    out_ref, gin_ref, gwin_hbm, gwout_hbm,
    win, wout, win_sib, wout_sib, xall, xsib,
    zsend, zrecv, own, ysend, yrecv, slope_ref, act,
    opart, xrecv, oown, osend, orecv, gwin, gwout,
    ssem, rsem, lsem,
):
    r, col = lax.axis_index("row"), lax.axis_index("col")
    y, zl, k = r // 4, (r // 2) % 2, r % 2
    x, zh = col // 4, col % 4

    def dev(dy=0, dzl=0, dk=0, dx=0, dzh=0):
        row = (((y + dy) % NY) * 2 + (zl + dzl) % 2) * 2 + (k + dk) % 2
        return (row, ((x + dx) % NX) * 4 + (zh + dzh) % NZH)

    partners = (
        [dev(dk=1), dev(dzl=1)]
        + [dev(dzh=d) for d in RING4]
        + [dev(dx=d) for d in RING4]
        + [dev(dy=d) for d in RING8]
    )
    count = [0]
    sent = []

    def send(src, dst, to):
        i = count[0]
        count[0] += 1
        copy = pltpu.make_async_remote_copy(
            src_ref=src, dst_ref=dst, send_sem=ssem.at[i], recv_sem=rsem.at[i],
            device_id=to, device_id_type=MESH,
        )
        copy.start()
        sent.append(copy)
        return copy

    mine = rows(col, CHUNK)
    own_in = [
        pltpu.make_async_copy(inp_hbm, xall.at[0, mine], lsem.at[4]),
        pltpu.make_async_copy(og_hbm, xall.at[1, mine], lsem.at[5]),
    ]
    for copy in own_in:
        copy.start()
    local = []
    for h in range(2):
        cols = pl.ds(h * HALF, HALF)
        local.append(pltpu.make_async_copy(win_hbm.at[:, cols], win.at[h], lsem.at[2 * h]))
        local.append(pltpu.make_async_copy(wout_hbm.at[cols, :], wout.at[h], lsem.at[2 * h + 1]))
    for copy in local:
        copy.start()

    barrier = pltpu.get_barrier_semaphore()
    for partner in partners:
        pl.semaphore_signal(barrier, inc=1, device_id=partner, device_id_type=MESH)
    pl.semaphore_wait(barrier, len(partners))

    a1 = [
        [send(ref, xall.at[a, mine], dev(dzh=d)) for d in RING4] for a, ref in enumerate((inp_hbm, og_hbm))
    ]
    other = rows(1 - k, HALF)
    s_win = send(win_hbm.at[:, other], win_sib, dev(dk=1))
    s_wout = send(wout_hbm.at[other, :], wout_sib, dev(dk=1))
    a2, a3 = [], []
    for a in range(2):
        own_in[a].wait()
        for copy in a1[a]:
            copy.wait_recv()
        block = rows(x, 64)
        a2.append([send(xall.at[a, block], xall.at[a, block], dev(dx=d)) for d in RING4])
        a3.append([send(xall.at[a, block], xsib.at[a, block], dev(dk=1))])
    for a in range(2):
        for d, copy in zip(RING4, a2[a]):
            copy.wait_recv()
            block = rows((x - d) % NX, 64)
            a3[a].append(send(xall.at[a, block], xsib.at[a, block], dev(dk=1)))

    for copy in local:
        copy.wait()
    s_win.wait_recv()
    s_wout.wait_recv()

    zcopy = []
    for a in range(2):
        for copy in a3[a]:
            copy.wait_recv()

        def chip_sum(half):
            block = rows(half, 128)
            if a == 0:
                return dot_nn(xall[a, block, :], win[k]) + dot_nn(xsib[a, block, :], win_sib[...])
            return dot_nt(xall[a, block, :], wout[k]) + dot_nt(xsib[a, block, :], wout_sib[...])

        zsend[a] = chip_sum(1 - zl).astype(BF16)
        zcopy.append(send(zsend.at[a], zrecv.at[a], dev(dzl=1)))
        own[a] = chip_sum(zl)

    ycopy = []
    for a in range(2):
        zcopy[a].wait_recv()
        copies = []
        for d in RING8:
            block = rows((y + d) % NY, CHUNK)
            ysend[a, d] = (own[a, block, :] + zrecv[a, block, :].astype(F32)).astype(BF16)
            copies.append(send(ysend.at[a, d], yrecv.at[a, d], dev(dy=d)))
        ycopy.append(copies)
    ccopy = []
    slot = rows(zl * NY + y, CHUNK)
    for a in range(2):
        block = rows(y, CHUNK)
        total = own[a, block, :] + zrecv[a, block, :].astype(F32)
        for d, copy in zip(RING8, ycopy[a]):
            copy.wait_recv()
            total = total + yrecv[a, d].astype(F32)
        if a == 0:
            hidden, slope = gelu_and_slope(total)
            slope_ref[...] = slope
            act[a, k, slot, :] = hidden.astype(BF16)
        else:
            act[a, k, slot, :] = (total * slope_ref[...]).astype(BF16)
        ref = act.at[a, k, slot]
        by_y = [send(ref, ref, dev(dy=d)) for d in RING8]
        by_z = [send(ref, ref, dev(dzl=1))]
        by_k = [send(ref, ref, dev(dk=1))]
        ccopy.append((by_y, by_z, by_k))

    for a in range(2):
        by_y, by_z, by_k = ccopy[a]
        for d, copy in zip(RING8, by_y):
            copy.wait_recv()
            ref = act.at[a, k, rows(zl * NY + (y - d) % NY, CHUNK)]
            by_z.append(send(ref, ref, dev(dzl=1)))
            by_k.append(send(ref, ref, dev(dk=1)))
        for d, copy in zip((0,) + RING8, by_z):
            copy.wait_recv()
            ref = act.at[a, k, rows((1 - zl) * NY + (y - d) % NY, CHUNK)]
            by_k.append(send(ref, ref, dev(dk=1)))

    xcopy = []
    for a in range(2):
        for copy in ccopy[a][2]:
            copy.wait_recv()
        if a == 0:
            total = dot_nn(act[a, 0], wout[0]) + dot_nn(act[a, 1], wout[1])
        else:
            total = dot_nt(act[a, 0], win[0]) + dot_nt(act[a, 1], win[1])
        oown[a] = total
        opart[a] = total.astype(BF16)
        xcopy.append([
            send(opart.at[a, rows((x + d) % NX, 64)], xrecv.at[a, d], dev(dx=d)) for d in RING4
        ])

    stores = []
    for h in range(2):
        gwout[h] = dot_tn(act[0, h], xall[1]).astype(BF16)
        copy = pltpu.make_async_copy(gwout.at[h], gwout_hbm.at[pl.ds(h * HALF, HALF), :], lsem.at[h])
        copy.start()
        stores.append(copy)

    ocopy = []
    for a in range(2):
        for copy in xcopy[a]:
            copy.wait_recv()
        total = oown[a, rows(x, 64), :]
        for d in RING4:
            total = total + xrecv[a, d].astype(F32)
        oown[a, rows(x, 64), :] = total
        osend[a] = total.astype(BF16)
        ocopy.append([
            send(osend.at[a, rows((zh + d) % NZH, CHUNK)], orecv.at[a, d], dev(dzh=d)) for d in RING4
        ])

    for h in range(2):
        gwin[h] = dot_tn(xall[0], act[1, h]).astype(BF16)
        copy = pltpu.make_async_copy(gwin.at[h], gwin_hbm.at[:, pl.ds(h * HALF, HALF)], lsem.at[2 + h])
        copy.start()
        stores.append(copy)

    for a, ref in enumerate((out_ref, gin_ref)):
        for copy in ocopy[a]:
            copy.wait_recv()
        total = oown[a, rows(col, CHUNK), :]
        for d in RING4:
            total = total + orecv[a, d].astype(F32)
        ref[...] = total.astype(BF16)

    for copy in stores:
        copy.wait()
    for copy in sent:
        copy.wait_send()


N_SENDS = 2 + 2 * (3 + 3 + 4 + 1 + 7 + 7 + 8 + 16 + 3 + 3)


def on_device(inputs, w_in, w_out, out_grad):
    vmem = pl.BlockSpec(memory_space=pltpu.VMEM)
    hbm = pl.BlockSpec(memory_space=pl.ANY)
    flops = 6 * 2 * TOK * FEAT * HID
    return pl.pallas_call(
        kernel,
        out_shape=(
            jax.ShapeDtypeStruct((CHUNK, FEAT), BF16),
            jax.ShapeDtypeStruct((CHUNK, FEAT), BF16),
            jax.ShapeDtypeStruct((FEAT, HID), BF16),
            jax.ShapeDtypeStruct((HID, FEAT), BF16),
        ),
        in_specs=[hbm, hbm, hbm, hbm],
        out_specs=(vmem, vmem, hbm, hbm),
        scratch_shapes=[
            pltpu.VMEM((2, FEAT, HALF), BF16),
            pltpu.VMEM((2, HALF, FEAT), BF16),
            pltpu.VMEM((FEAT, HALF), BF16),
            pltpu.VMEM((HALF, FEAT), BF16),
            pltpu.VMEM((2, TOK, FEAT), BF16),
            pltpu.VMEM((2, TOK, FEAT), BF16),
            pltpu.VMEM((2, 128, HALF), BF16),
            pltpu.VMEM((2, 128, HALF), BF16),
            pltpu.VMEM((2, 128, HALF), F32),
            pltpu.VMEM((2, NY, CHUNK, HALF), BF16),
            pltpu.VMEM((2, NY, CHUNK, HALF), BF16),
            pltpu.VMEM((CHUNK, HALF), F32),
            pltpu.VMEM((2, 2, TOK, HALF), BF16),
            pltpu.VMEM((2, TOK, FEAT), BF16),
            pltpu.VMEM((2, NX, 64, FEAT), BF16),
            pltpu.VMEM((2, TOK, FEAT), F32),
            pltpu.VMEM((2, 64, FEAT), BF16),
            pltpu.VMEM((2, NZH, CHUNK, FEAT), BF16),
            pltpu.VMEM((2, FEAT, HALF), BF16),
            pltpu.VMEM((2, HALF, FEAT), BF16),
            pltpu.SemaphoreType.DMA((N_SENDS,)),
            pltpu.SemaphoreType.DMA((N_SENDS,)),
            pltpu.SemaphoreType.DMA((6,)),
        ],
        compiler_params=pltpu.CompilerParams(
            collective_id=0, has_side_effects=True, vmem_limit_bytes=60 * 1024 * 1024
        ),
        cost_estimate=pl.CostEstimate(flops=flops, bytes_accessed=4 * 2 * FEAT * HID, transcendentals=CHUNK * HALF),
        name="mlp_block",
    )(inputs, out_grad, w_in, w_out)


def solution(mesh):
    return jax.shard_map(
        on_device,
        mesh=mesh,
        in_specs=(P("col", "row"), P("row", "col"), P("col", "row"), P("col", "row")),
        out_specs=(P("col", "row"), P("col", "row"), P("row", "col"), P("col", "row")),
        check_vma=False,
    )
```

```python
import jax
import jax.numpy as jnp
from jax import lax
from jax.experimental import pallas as pl
from jax.experimental.pallas import tpu as pltpu
from jax.sharding import PartitionSpec as P

MESH = pl.DeviceIdType.MESH
BF16, F32 = jnp.bfloat16, jnp.float32
NY, NZL, NK, NX, NZH = 8, 2, 2, 4, 4
TOK, FEAT, HID, HALF = 256, 384, 1536, 768
CHUNK = 16
RING8 = (4, 3, 5, 2, 6, 1, 7)
RING4 = (2, 1, 3)

gelu_coef = 0.7978845608028654


def gelu_and_slope(value):
    inner = gelu_coef * (value + 0.044715 * value * value * value)
    tanh_val = jnp.tanh(inner)
    gelu = 0.5 * value * (1.0 + tanh_val)
    slope = 0.5 * (1.0 + tanh_val) + 0.5 * value * (1.0 - tanh_val * tanh_val) * gelu_coef * (
        1.0 + 3.0 * 0.044715 * value * value
    )
    return gelu, slope


def dot_nn(a, b):
    return lax.dot_general(a, b, (((1,), (0,)), ((), ())), preferred_element_type=F32)


def dot_nt(a, b):
    return lax.dot_general(a, b, (((1,), (1,)), ((), ())), preferred_element_type=F32)


def dot_tn(a, b):
    return lax.dot_general(a, b, (((0,), (0,)), ((), ())), preferred_element_type=F32)


def rows(index, size):
    return pl.ds(pl.multiple_of(index * size, size), size)


def kernel(
    inp_hbm, og_hbm, win_hbm, wout_hbm,
    out_ref, gin_ref, gwin_ref, gwout_ref,
    win, wout, win_sib, wout_sib, xall, xsib,
    zsend, zrecv, own, ysend, yrecv, slope_ref, act,
    opart, xrecv, oown, osend, orecv,
    ssem, rsem, lsem,
):
    r, col = lax.axis_index("row"), lax.axis_index("col")
    y, zl, k = r // 4, (r // 2) % 2, r % 2
    x, zh = col // 4, col % 4

    def dev(dy=0, dzl=0, dk=0, dx=0, dzh=0):
        row = (((y + dy) % NY) * 2 + (zl + dzl) % 2) * 2 + (k + dk) % 2
        return (row, ((x + dx) % NX) * 4 + (zh + dzh) % NZH)

    partners = (
        [dev(dk=1), dev(dzl=1)]
        + [dev(dzh=d) for d in RING4]
        + [dev(dx=d) for d in RING4]
        + [dev(dy=d) for d in RING8]
    )
    count = [0]
    sent = []

    def send(src, dst, to):
        i = count[0]
        count[0] += 1
        copy = pltpu.make_async_remote_copy(
            src_ref=src, dst_ref=dst, send_sem=ssem.at[i], recv_sem=rsem.at[i],
            device_id=to, device_id_type=MESH,
        )
        copy.start()
        sent.append(copy)
        return copy

    own_in = [
        pltpu.make_async_copy(inp_hbm, xall.at[0, x, zh], lsem.at[4]),
        pltpu.make_async_copy(og_hbm, xall.at[1, x, zh], lsem.at[5]),
    ]
    for copy in own_in:
        copy.start()
    local = []
    for h in range(2):
        cols = pl.ds(h * HALF, HALF)
        local.append(pltpu.make_async_copy(win_hbm.at[:, cols], win.at[h], lsem.at[2 * h]))
        local.append(pltpu.make_async_copy(wout_hbm.at[cols, :], wout.at[h], lsem.at[2 * h + 1]))
    for copy in local:
        copy.start()

    barrier = pltpu.get_barrier_semaphore()
    for partner in partners:
        pl.semaphore_signal(barrier, inc=1, device_id=partner, device_id_type=MESH)
    pl.semaphore_wait(barrier, len(partners))

    shards = (inp_hbm, og_hbm)
    by_zh = [[send(ref, xall.at[a, x, zh], dev(dzh=d)) for d in RING4] for a, ref in enumerate(shards)]
    by_x = [[[send(ref, xall.at[a, x, zh], dev(dx=d)) for d in RING4]] for a, ref in enumerate(shards)]
    other = rows(1 - k, HALF)
    s_win = send(win_hbm.at[:, other], win_sib, dev(dk=1))
    s_wout = send(wout_hbm.at[other, :], wout_sib, dev(dk=1))
    for i, d in enumerate(RING4):
        for a in range(2):
            by_zh[a][i].wait_recv()
            ref = xall.at[a, x, (zh - d) % NZH]
            by_x[a].append([send(ref, ref, dev(dx=e)) for e in RING4])

    def pass_to_core(a):
        copies = []
        for d, group in zip((0,) + RING4, by_x[a]):
            if d == 0:
                own_in[a].wait()
            for copy in group:
                copy.wait_recv()
            part = (zh - d) % NZH
            copies.append(send(xall.at[a, :, part], xsib.at[a, :, part], dev(dk=1)))
        return copies

    def chip_sum(a, half):
        block = pl.ds(half * (NX // 2), NX // 2)
        mine, theirs = (ref[a, block].reshape(128, FEAT) for ref in (xall, xsib))
        if a == 0:
            return dot_nn(mine, win[k]) + dot_nn(theirs, win_sib[...])
        return dot_nt(mine, wout[k]) + dot_nt(theirs, wout_sib[...])

    def send_over_z(a):
        zsend[a] = chip_sum(a, 1 - zl).astype(BF16)
        copies = []
        for d in RING8 + (0,):
            block = rows((y + d) % NY, CHUNK)
            copies.append(send(zsend.at[a, block], zrecv.at[a, block], dev(dzl=1)))
        return copies

    def send_over_y(a, zcopy):
        copies = []
        for d, copy in zip(RING8, zcopy):
            copy.wait_recv()
            block = rows((y + d) % NY, CHUNK)
            ysend[a, d] = (own[a, block, :] + zrecv[a, block, :].astype(F32)).astype(BF16)
            copies.append(send(ysend.at[a, d], yrecv.at[a, d], dev(dy=d)))
        return copies

    a3 = pass_to_core(0)
    for copy in local:
        copy.wait()
    s_win.wait_recv()
    for copy in a3:
        copy.wait_recv()
    z0 = send_over_z(0)
    a3 = pass_to_core(1)
    own[0] = chip_sum(0, zl)
    s_wout.wait_recv()
    for copy in a3:
        copy.wait_recv()
    z1 = send_over_z(1)
    y0 = send_over_y(0, z0)
    own[1] = chip_sum(1, zl)
    y1 = send_over_y(1, z1)

    def chunk(a, half, d):
        return act.at[a, k, rows(half * NY + (y + d) % NY, CHUNK)]

    def finish_sum(a, zlast, ycopy):
        zlast.wait_recv()
        block = rows(y, CHUNK)
        total = own[a, block, :] + zrecv[a, block, :].astype(F32)
        for d, copy in zip(RING8, ycopy):
            copy.wait_recv()
            total = total + yrecv[a, d].astype(F32)
        slot = rows(zl * NY + y, CHUNK)
        if a == 0:
            hidden, slope = gelu_and_slope(total)
            slope_ref[...] = slope
            act[a, k, slot, :] = hidden.astype(BF16)
        else:
            act[a, k, slot, :] = (total * slope_ref[...]).astype(BF16)
        ref = chunk(a, zl, 0)
        near = [send(ref, ref, dev(dy=d)) for d in (2, -2, 1, -1)]
        return near, [send(ref, ref, dev(dzl=1))]

    def pass_near(a):
        near, over_z = ccopy[a]
        near[0].wait_recv()
        near[1].wait_recv()
        left, right, far = chunk(a, zl, -2), chunk(a, zl, 2), chunk(a, zl, -2 * turn)
        last = [send(far, far, dev(dy=2 * turn)), send(left, left, dev(dy=1)), send(right, right, dev(dy=-1))]
        over_z += [send(ref, ref, dev(dzl=1)) for ref in (left, right)]
        near[2].wait_recv()
        near[3].wait_recv()
        over_z += [send(ref, ref, dev(dzl=1)) for ref in (chunk(a, zl, -1), chunk(a, zl, 1))]
        return last

    def pass_last(a, last):
        for d, copy in zip((4, -3, 3), last):
            copy.wait_recv()
            ref = chunk(a, zl, d)
            ccopy[a][1].append(send(ref, ref, dev(dzl=1)))
        ref = act.at[a, k, rows(zl, 128)]
        return [send(ref, ref, dev(dk=1))]

    def pass_from_z(a, by_k):
        for d, copy in zip((0, -2, 2, -1, 1, 4, -3, 3), ccopy[a][1]):
            copy.wait_recv()
            ref = chunk(a, 1 - zl, d)
            by_k.append(send(ref, ref, dev(dk=1)))

    def send_over_x(a, by_k):
        for copy in by_k:
            copy.wait_recv()
        if a == 0:
            total = dot_nn(act[a, 0], wout[0]) + dot_nn(act[a, 1], wout[1])
        else:
            total = dot_nt(act[a, 0], win[0]) + dot_nt(act[a, 1], win[1])
        total = total.reshape(NX, NZH, CHUNK, FEAT)
        oown[a] = total
        opart[a] = total.astype(BF16)
        return [
            [
                send(opart.at[a, (x + e) % NX, (zh + d) % NZH], xrecv.at[a, d, e], dev(dx=e))
                for e in RING4
            ]
            for d in RING4 + (0,)
        ]

    def sum_over_x(a, d, copies):
        total = oown[a, x, (zh + d) % NZH]
        for e, copy in zip(RING4, copies):
            copy.wait_recv()
            total = total + xrecv[a, d, e].astype(F32)
        return total

    def send_over_zh(a, xcopy):
        copies = []
        for d, group in zip(RING4, xcopy):
            osend[a, d] = sum_over_x(a, d, group)
            copies.append(send(osend.at[a, d], orecv.at[a, d], dev(dzh=d)))
        return copies

    turn = 1 - 2 * (y % 2)
    ccopy = [finish_sum(0, z0[7], y0)]
    ccopy.append(finish_sum(1, z1[7], y1))
    last0 = pass_near(0)
    last1 = pass_near(1)
    k0 = pass_last(0, last0)
    k1 = pass_last(1, last1)
    pass_from_z(0, k0)
    x0 = send_over_x(0, k0)
    pass_from_z(1, k1)
    x1 = send_over_x(1, k1)
    o0 = send_over_zh(0, x0)
    for h in range(2):
        gwout_ref[pl.ds(h * HALF, HALF), :] = dot_tn(act[0, h], xall[1].reshape(TOK, FEAT)).astype(BF16)
    o1 = send_over_zh(1, x1)
    for h in range(2):
        gwin_ref[:, pl.ds(h * HALF, HALF)] = dot_tn(xall[0].reshape(TOK, FEAT), act[1, h]).astype(BF16)
    for a, (ref, xcopy, copies) in enumerate(((out_ref, x0, o0), (gin_ref, x1, o1))):
        total = sum_over_x(a, 0, xcopy[3])
        for d, copy in zip(RING4, copies):
            copy.wait_recv()
            total = total + orecv[a, d]
        ref[...] = total.astype(BF16)

    for copy in sent:
        copy.wait_send()


N_SENDS = 2 + 2 * (3 + 12 + 4 + 8 + 7 + 7 + 8 + 9 + 12 + 3)


def place(*refs):
    parts = []
    n, sem = (len(refs) - 1) // 2, refs[-1]
    for i in range(n):
        parts.append(pltpu.make_async_copy(refs[i], refs[n + i], sem.at[i]))
        parts[-1].start()
    for part in parts:
        part.wait()


def on_device(inputs, w_in, w_out, out_grad):
    shapes = (
        jax.ShapeDtypeStruct((CHUNK, FEAT), BF16),
        jax.ShapeDtypeStruct((CHUNK, FEAT), BF16),
        jax.ShapeDtypeStruct((FEAT, HID), BF16),
        jax.ShapeDtypeStruct((HID, FEAT), BF16),
    )
    vmem = pl.BlockSpec(memory_space=pltpu.VMEM)
    hbm = pl.BlockSpec(memory_space=pl.ANY)
    flops = 6 * 2 * TOK * FEAT * HID
    results = pl.pallas_call(
        kernel,
        out_shape=shapes,
        in_specs=[hbm, hbm, hbm, hbm],
        out_specs=(vmem, vmem, vmem, vmem),
        scratch_shapes=[
            pltpu.VMEM((2, FEAT, HALF), BF16),
            pltpu.VMEM((2, HALF, FEAT), BF16),
            pltpu.VMEM((FEAT, HALF), BF16),
            pltpu.VMEM((HALF, FEAT), BF16),
            pltpu.VMEM((2, NX, NZH, CHUNK, FEAT), BF16),
            pltpu.VMEM((2, NX, NZH, CHUNK, FEAT), BF16),
            pltpu.VMEM((2, 128, HALF), BF16),
            pltpu.VMEM((2, 128, HALF), BF16),
            pltpu.VMEM((2, 128, HALF), F32),
            pltpu.VMEM((2, NY, CHUNK, HALF), BF16),
            pltpu.VMEM((2, NY, CHUNK, HALF), BF16),
            pltpu.VMEM((CHUNK, HALF), F32),
            pltpu.VMEM((2, 2, TOK, HALF), BF16),
            pltpu.VMEM((2, NX, NZH, CHUNK, FEAT), BF16),
            pltpu.VMEM((2, NZH, NX, CHUNK, FEAT), BF16),
            pltpu.VMEM((2, NX, NZH, CHUNK, FEAT), F32),
            pltpu.VMEM((2, NZH, CHUNK, FEAT), F32),
            pltpu.VMEM((2, NZH, CHUNK, FEAT), F32),
            pltpu.SemaphoreType.DMA((N_SENDS,)),
            pltpu.SemaphoreType.DMA((N_SENDS,)),
            pltpu.SemaphoreType.DMA((6,)),
        ],
        compiler_params=pltpu.CompilerParams(
            collective_id=0, has_side_effects=True, vmem_limit_bytes=40 * 1024 * 1024
        ),
        cost_estimate=pl.CostEstimate(flops=flops, bytes_accessed=4 * 2 * FEAT * HID, transcendentals=CHUNK * HALF),
        name="mlp_block",
    )(*(pltpu.with_memory_space_constraint(v, pltpu.HBM) for v in (inputs, out_grad, w_in, w_out)))
    return pl.pallas_call(
        place,
        out_shape=shapes,
        in_specs=[hbm] * 4,
        out_specs=[hbm] * 4,
        scratch_shapes=[pltpu.SemaphoreType.DMA((4,))],
        compiler_params=pltpu.CompilerParams(vmem_limit_bytes=4 * 1024 * 1024),
        name="place_results",
    )(*results)


def solution(mesh):
    return jax.shard_map(
        on_device,
        mesh=mesh,
        in_specs=(P("col", "row"), P("row", "col"), P("col", "row"), P("col", "row")),
        out_specs=(P("col", "row"), P("col", "row"), P("row", "col"), P("col", "row")),
        check_vma=False,
    )
```

```python
import jax
import jax.numpy as jnp
from jax import lax
from jax.experimental import pallas as pl
from jax.experimental.pallas import tpu as pltpu
from jax.sharding import PartitionSpec as P

MESH = pl.DeviceIdType.MESH
BF16, F32 = jnp.bfloat16, jnp.float32
NY, NZL, NK, NX, NZH = 8, 2, 2, 4, 4
TOK, FEAT, HID, HALF = 256, 384, 1536, 768
CHUNK = 16
RING8 = (4, 3, 5, 2, 6, 1, 7)
RING4 = (2, 1, 3)

gelu_coef = 0.7978845608028654


def gelu_and_slope(value):
    inner = gelu_coef * (value + 0.044715 * value * value * value)
    tanh_val = jnp.tanh(inner)
    gelu = 0.5 * value * (1.0 + tanh_val)
    slope = 0.5 * (1.0 + tanh_val) + 0.5 * value * (1.0 - tanh_val * tanh_val) * gelu_coef * (
        1.0 + 3.0 * 0.044715 * value * value
    )
    return gelu, slope


def dot_nn(a, b):
    return lax.dot_general(a, b, (((1,), (0,)), ((), ())), preferred_element_type=F32)


def dot_nt(a, b):
    return lax.dot_general(a, b, (((1,), (1,)), ((), ())), preferred_element_type=F32)


def dot_tn(a, b):
    return lax.dot_general(a, b, (((0,), (0,)), ((), ())), preferred_element_type=F32)


def rows(index, size):
    return pl.ds(pl.multiple_of(index * size, size), size)


def kernel(
    inp_hbm, og_hbm, win_hbm, wout_hbm,
    out_ref, gin_ref, gwin_ref, gwout_ref,
    win, wout, win_sib, wout_sib, xall, xsib,
    part, zsend, zrecv, own, ysend, yrecv, slope_ref, act,
    opart, xrecv, oacc, oown, osend, orecv,
    ssem, rsem, lsem,
):
    r, col = lax.axis_index("row"), lax.axis_index("col")
    y, zl, k = r // 4, (r // 2) % 2, r % 2
    x, zh = col // 4, col % 4

    def dev(dy=0, dzl=0, dk=0, dx=0, dzh=0):
        row = (((y + dy) % NY) * 2 + (zl + dzl) % 2) * 2 + (k + dk) % 2
        return (row, ((x + dx) % NX) * 4 + (zh + dzh) % NZH)

    partners = (
        [dev(dk=1), dev(dzl=1)]
        + [dev(dzh=d) for d in RING4]
        + [dev(dx=d) for d in RING4]
        + [dev(dy=d) for d in RING8]
        + [dev(dy=d, dzl=1) for d in (1, -1, 2, -2)]
    )
    count = [0]
    sent = []

    def send(src, dst, to):
        i = count[0]
        count[0] += 1
        copy = pltpu.make_async_remote_copy(
            src_ref=src, dst_ref=dst, send_sem=ssem.at[i], recv_sem=rsem.at[i],
            device_id=to, device_id_type=MESH,
        )
        copy.start()
        sent.append(copy)
        return copy

    own_in = [
        pltpu.make_async_copy(inp_hbm, xall.at[0, x, zh], lsem.at[4]),
        pltpu.make_async_copy(og_hbm, xall.at[1, x, zh], lsem.at[5]),
    ]
    for copy in own_in:
        copy.start()
    local = []
    for h in range(2):
        cols = pl.ds(h * HALF, HALF)
        local.append(pltpu.make_async_copy(win_hbm.at[:, cols], win.at[h], lsem.at[2 * h]))
        local.append(pltpu.make_async_copy(wout_hbm.at[cols, :], wout.at[h], lsem.at[2 * h + 1]))
    for copy in local:
        copy.start()

    barrier = pltpu.get_barrier_semaphore()
    for partner in partners:
        pl.semaphore_signal(barrier, inc=1, device_id=partner, device_id_type=MESH)
    pl.semaphore_wait(barrier, len(partners))

    shards = (inp_hbm, og_hbm)

    def send_shard(a, over):
        return [send(shards[a], xall.at[a, x, zh], dev(**{over: d})) for d in RING4]

    by_zh = [send_shard(0, "dzh")]
    by_x = [[send_shard(0, "dx")]]
    by_zh.append(send_shard(1, "dzh"))
    other = rows(1 - k, HALF)
    s_win = send(win_hbm.at[:, other], win_sib, dev(dk=1))
    s_wout = send(wout_hbm.at[other, :], wout_sib, dev(dk=1))
    for a in range(2):
        if a == 1:
            by_x.append([send_shard(1, "dx")])
        for d in (1, 3, 2):
            by_zh[a][RING4.index(d)].wait_recv()
            ref = xall.at[a, x, (zh - d) % NZH]
            by_x[a].append([send(ref, ref, dev(dx=e)) for e in RING4])

    def pass_to_core(a):
        copies = []
        for d, group in zip((0, 1, 3, 2), by_x[a]):
            if d == 0:
                own_in[a].wait()
            for copy in group:
                copy.wait_recv()
            part = (zh - d) % NZH
            copies.append(send(xall.at[a, :, part], xsib.at[a, :, part], dev(dk=1)))
        return copies

    def own_features(a):
        mine = xall[a].reshape(TOK, FEAT)
        part[a] = dot_nn(mine, win[k]) if a == 0 else dot_nt(mine, wout[k])

    def chip_sum(a, half):
        theirs = xsib[a, pl.ds(half * (NX // 2), NX // 2)].reshape(128, FEAT)
        more = dot_nn(theirs, win_sib[...]) if a == 0 else dot_nt(theirs, wout_sib[...])
        return part[a, rows(half, 128), :] + more

    def send_over_z(a):
        zsend[a] = chip_sum(a, 1 - zl).astype(BF16)
        copies = []
        for d in RING8 + (0,):
            block = rows((y + d) % NY, CHUNK)
            copies.append(send(zsend.at[a, block], zrecv.at[a, block], dev(dzl=1)))
        return copies

    def send_over_y(a, zcopy):
        copies = []
        for d, copy in zip(RING8, zcopy):
            copy.wait_recv()
            block = rows((y + d) % NY, CHUNK)
            ysend[a, d] = (own[a, block, :] + zrecv[a, block, :].astype(F32)).astype(BF16)
            copies.append(send(ysend.at[a, d], yrecv.at[a, d], dev(dy=d)))
        return copies

    a3 = pass_to_core(0)
    for copy in local:
        copy.wait()
    own_features(0)
    s_win.wait_recv()
    for copy in a3:
        copy.wait_recv()
    z0 = send_over_z(0)
    a3 = pass_to_core(1)
    own[0] = chip_sum(0, zl)
    own_features(1)
    s_wout.wait_recv()
    for copy in a3:
        copy.wait_recv()
    z1 = send_over_z(1)
    y0 = send_over_y(0, z0)
    own[1] = chip_sum(1, zl)
    y1 = send_over_y(1, z1)

    def chunk(a, half, d):
        return act.at[a, k, rows(half * NY + (y + d) % NY, CHUNK)]

    def finish_sum(a, zlast, ycopy):
        zlast.wait_recv()
        block = rows(y, CHUNK)
        total = own[a, block, :] + zrecv[a, block, :].astype(F32)
        for d, copy in zip(RING8, ycopy):
            copy.wait_recv()
            total = total + yrecv[a, d].astype(F32)
        slot = rows(zl * NY + y, CHUNK)
        if a == 0:
            hidden, slope = gelu_and_slope(total)
            slope_ref[...] = slope
            act[a, k, slot, :] = hidden.astype(BF16)
        else:
            act[a, k, slot, :] = (total * slope_ref[...]).astype(BF16)
        ref = chunk(a, zl, 0)
        near = {d: send(ref, ref, dev(dy=d)) for d in (2, -2, 1, -1)}
        over_z = {0: send(ref, ref, dev(dzl=1))}
        return near, over_z, [send(ref, ref, dev(dk=1))]

    def pass_on(a, ref):
        ccopy[a][2].append(send(ref, ref, dev(dk=1)))

    def pass_near(a):
        near, over_z, _ = ccopy[a]
        near[2].wait_recv()
        near[-2].wait_recv()
        left, right, far = chunk(a, zl, -2), chunk(a, zl, 2), chunk(a, zl, -2 * turn)
        last = []
        for ref, d in ((far, 2 * turn), (left, 1), (right, -1)):
            last.append([send(ref, ref, dev(dy=d, dzl=dzl)) for dzl in (1, 0)])
        for d in (-2, 2, -1, 1):
            if abs(d) == 1:
                near[-d].wait_recv()
            ref = chunk(a, zl, d)
            over_z[d] = send(ref, ref, dev(dzl=1))
            pass_on(a, ref)
        return last

    def pass_last(a, last):
        for d in (0, -2, 2, -1, 1):
            ccopy[a][1][d].wait_recv()
            pass_on(a, chunk(a, 1 - zl, d))
        for d, (other_z, same_z) in zip((4, -3, 3), last):
            same_z.wait_recv()
            pass_on(a, chunk(a, zl, d))
            other_z.wait_recv()
            pass_on(a, chunk(a, 1 - zl, d))

    def model_width(a, half):
        return dot_nn(act[a, half], wout[half]) if a == 0 else dot_nt(act[a, half], win[half])

    def send_over_x(a):
        oacc[...] = model_width(a, k)
        for copy in ccopy[a][2]:
            copy.wait_recv()
        total = oacc[...] + model_width(a, 1 - k)
        total = total.reshape(NX, NZH, CHUNK, FEAT)
        oown[a] = total
        opart[a] = total.astype(BF16)
        return [
            [
                send(opart.at[a, (x + e) % NX, (zh + d) % NZH], xrecv.at[a, d, e], dev(dx=e))
                for e in RING4
            ]
            for d in RING4 + (0,)
        ]

    def sum_over_x(a, d, copies):
        total = oown[a, x, (zh + d) % NZH]
        for e, copy in zip(RING4, copies):
            copy.wait_recv()
            total = total + xrecv[a, d, e].astype(F32)
        return total

    def send_over_zh(a, xcopy):
        copies = []
        for d, group in zip(RING4, xcopy):
            osend[a, d] = sum_over_x(a, d, group)
            copies.append(send(osend.at[a, d], orecv.at[a, d], dev(dzh=d)))
        return copies

    turn = 1 - 2 * (y % 2)
    ccopy = [finish_sum(0, z0[7], y0)]
    ccopy.append(finish_sum(1, z1[7], y1))
    last0 = pass_near(0)
    last1 = pass_near(1)
    pass_last(0, last0)
    x0 = send_over_x(0)
    pass_last(1, last1)
    x1 = send_over_x(1)
    o0 = send_over_zh(0, x0)
    for h in range(2):
        gwout_ref[pl.ds(h * HALF, HALF), :] = dot_tn(act[0, h], xall[1].reshape(TOK, FEAT)).astype(BF16)
    o1 = send_over_zh(1, x1)
    for h in range(2):
        gwin_ref[:, pl.ds(h * HALF, HALF)] = dot_tn(xall[0].reshape(TOK, FEAT), act[1, h]).astype(BF16)
    for a, (ref, xcopy, copies) in enumerate(((out_ref, x0, o0), (gin_ref, x1, o1))):
        total = sum_over_x(a, 0, xcopy[3])
        for d, copy in zip(RING4, copies):
            copy.wait_recv()
            total = total + orecv[a, d]
        ref[...] = total.astype(BF16)

    for copy in sent:
        copy.wait_send()


N_SENDS = 2 + 2 * (3 + 12 + 4 + 8 + 7 + 4 + 6 + 5 + 16 + 12 + 3)


def place(*refs):
    parts = []
    n, sem = (len(refs) - 1) // 2, refs[-1]
    for i in range(n):
        parts.append(pltpu.make_async_copy(refs[i], refs[n + i], sem.at[i]))
        parts[-1].start()
    for part in parts:
        part.wait()


def on_device(inputs, w_in, w_out, out_grad):
    shapes = (
        jax.ShapeDtypeStruct((CHUNK, FEAT), BF16),
        jax.ShapeDtypeStruct((CHUNK, FEAT), BF16),
        jax.ShapeDtypeStruct((FEAT, HID), BF16),
        jax.ShapeDtypeStruct((HID, FEAT), BF16),
    )
    vmem = pl.BlockSpec(memory_space=pltpu.VMEM)
    hbm = pl.BlockSpec(memory_space=pl.ANY)
    flops = 6 * 2 * TOK * FEAT * HID
    results = pl.pallas_call(
        kernel,
        out_shape=shapes,
        in_specs=[hbm, hbm, hbm, hbm],
        out_specs=(vmem, vmem, vmem, vmem),
        scratch_shapes=[
            pltpu.VMEM((2, FEAT, HALF), BF16),
            pltpu.VMEM((2, HALF, FEAT), BF16),
            pltpu.VMEM((FEAT, HALF), BF16),
            pltpu.VMEM((HALF, FEAT), BF16),
            pltpu.VMEM((2, NX, NZH, CHUNK, FEAT), BF16),
            pltpu.VMEM((2, NX, NZH, CHUNK, FEAT), BF16),
            pltpu.VMEM((2, TOK, HALF), F32),
            pltpu.VMEM((2, 128, HALF), BF16),
            pltpu.VMEM((2, 128, HALF), BF16),
            pltpu.VMEM((2, 128, HALF), F32),
            pltpu.VMEM((2, NY, CHUNK, HALF), BF16),
            pltpu.VMEM((2, NY, CHUNK, HALF), BF16),
            pltpu.VMEM((CHUNK, HALF), F32),
            pltpu.VMEM((2, 2, TOK, HALF), BF16),
            pltpu.VMEM((2, NX, NZH, CHUNK, FEAT), BF16),
            pltpu.VMEM((2, NZH, NX, CHUNK, FEAT), BF16),
            pltpu.VMEM((TOK, FEAT), F32),
            pltpu.VMEM((2, NX, NZH, CHUNK, FEAT), F32),
            pltpu.VMEM((2, NZH, CHUNK, FEAT), F32),
            pltpu.VMEM((2, NZH, CHUNK, FEAT), F32),
            pltpu.SemaphoreType.DMA((N_SENDS,)),
            pltpu.SemaphoreType.DMA((N_SENDS,)),
            pltpu.SemaphoreType.DMA((6,)),
        ],
        compiler_params=pltpu.CompilerParams(
            collective_id=0, has_side_effects=True, vmem_limit_bytes=40 * 1024 * 1024
        ),
        cost_estimate=pl.CostEstimate(flops=flops, bytes_accessed=4 * 2 * FEAT * HID, transcendentals=CHUNK * HALF),
        name="mlp_block",
    )(*(pltpu.with_memory_space_constraint(v, pltpu.HBM) for v in (inputs, out_grad, w_in, w_out)))
    return pl.pallas_call(
        place,
        out_shape=shapes,
        in_specs=[hbm] * 4,
        out_specs=[hbm] * 4,
        scratch_shapes=[pltpu.SemaphoreType.DMA((4,))],
        compiler_params=pltpu.CompilerParams(vmem_limit_bytes=4 * 1024 * 1024),
        name="place_results",
    )(*results)


def solution(mesh):
    return jax.shard_map(
        on_device,
        mesh=mesh,
        in_specs=(P("col", "row"), P("row", "col"), P("col", "row"), P("col", "row")),
        out_specs=(P("col", "row"), P("col", "row"), P("row", "col"), P("col", "row")),
        check_vma=False,
    )
```

```python
import jax
import jax.numpy as jnp
from jax import lax
from jax.experimental import pallas as pl
from jax.experimental.pallas import tpu as pltpu
from jax.sharding import PartitionSpec as P

MESH = pl.DeviceIdType.MESH
BF16, F32 = jnp.bfloat16, jnp.float32
NY, NZL, NK, NX, NZH = 8, 2, 2, 4, 4
TOK, FEAT, HID, HALF = 256, 384, 1536, 768
CHUNK = 16
RING8 = (4, 3, 5, 2, 6, 1, 7)
RING4 = (2, 1, 3)

gelu_coef = 0.7978845608028654


def gelu_and_slope(value):
    inner = gelu_coef * (value + 0.044715 * value * value * value)
    tanh_val = jnp.tanh(inner)
    gelu = 0.5 * value * (1.0 + tanh_val)
    slope = 0.5 * (1.0 + tanh_val) + 0.5 * value * (1.0 - tanh_val * tanh_val) * gelu_coef * (
        1.0 + 3.0 * 0.044715 * value * value
    )
    return gelu, slope


def dot_nn(a, b):
    return lax.dot_general(a, b, (((1,), (0,)), ((), ())), preferred_element_type=F32)


def dot_nt(a, b):
    return lax.dot_general(a, b, (((1,), (1,)), ((), ())), preferred_element_type=F32)


def dot_tn(a, b):
    return lax.dot_general(a, b, (((0,), (0,)), ((), ())), preferred_element_type=F32)


def rows(index, size):
    return pl.ds(pl.multiple_of(index * size, size), size)


def kernel(
    inp_hbm, og_hbm, win_hbm, wout_hbm,
    out_ref, gin_ref, gwin_ref, gwout_ref,
    win, wout, win_sib, wout_sib, xall, xsib,
    part, zsend, zrecv, own, ysend, yrecv, slope_ref, act,
    opart, xrecv, oacc, oown, osend, orecv,
    ssem, rsem, lsem,
):
    r, col = lax.axis_index("row"), lax.axis_index("col")
    y, zl, k = r // 4, (r // 2) % 2, r % 2
    x, zh = col // 4, col % 4

    def dev(dy=0, dzl=0, dk=0, dx=0, dzh=0):
        row = (((y + dy) % NY) * 2 + (zl + dzl) % 2) * 2 + (k + dk) % 2
        return (row, ((x + dx) % NX) * 4 + (zh + dzh) % NZH)

    partners = (
        [dev(dzh=2), dev(dy=4), dev(dy=3), dev(dy=-3)]
        + [dev(dzh=d) for d in (1, 3)]
        + [dev(dy=d, dzl=1) for d in (2, -2)]
        + [dev(dy=d) for d in (2, -2)]
        + [dev(dx=d) for d in RING4]
        + [dev(dy=d, dzl=1) for d in (1, -1)]
        + [dev(dy=d) for d in (1, -1)]
        + [dev(dzl=1), dev(dk=1)]
    )
    barrier = pltpu.get_barrier_semaphore()
    for partner in partners:
        pl.semaphore_signal(barrier, inc=1, device_id=partner, device_id_type=MESH)
    count = [0]
    sent = []

    def send(src, dst, to):
        i = count[0]
        count[0] += 1
        copy = pltpu.make_async_remote_copy(
            src_ref=src, dst_ref=dst, send_sem=ssem.at[i], recv_sem=rsem.at[i],
            device_id=to, device_id_type=MESH,
        )
        copy.start()
        sent.append(copy)
        return copy

    own_in = [
        pltpu.make_async_copy(inp_hbm, xall.at[0, x, zh], lsem.at[4]),
        pltpu.make_async_copy(og_hbm, xall.at[1, x, zh], lsem.at[5]),
    ]
    for copy in own_in:
        copy.start()
    local = []
    for h in range(2):
        cols = pl.ds(h * HALF, HALF)
        local.append(pltpu.make_async_copy(win_hbm.at[:, cols], win.at[h], lsem.at[2 * h]))
        local.append(pltpu.make_async_copy(wout_hbm.at[cols, :], wout.at[h], lsem.at[2 * h + 1]))
    for copy in local:
        copy.start()

    pl.semaphore_wait(barrier, len(partners))

    shards = (inp_hbm, og_hbm)

    def send_shard(a, over):
        return [send(shards[a], xall.at[a, x, zh], dev(**{over: d})) for d in RING4]

    by_zh = [send_shard(0, "dzh")]
    by_x = [[send_shard(0, "dx")]]
    by_zh.append(send_shard(1, "dzh"))
    other = rows(1 - k, HALF)
    s_win = send(win_hbm.at[:, other], win_sib, dev(dk=1))
    s_wout = send(wout_hbm.at[other, :], wout_sib, dev(dk=1))
    for a in range(2):
        if a == 1:
            by_x.append([send_shard(1, "dx")])
        for d in (1, 3, 2):
            by_zh[a][RING4.index(d)].wait_recv()
            ref = xall.at[a, x, (zh - d) % NZH]
            by_x[a].append([send(ref, ref, dev(dx=e)) for e in RING4])

    def pass_to_core(a):
        own_in[a].wait()
        for group in by_x[a]:
            for copy in group:
                copy.wait_recv()
        return [send(xall.at[a], xsib.at[a], dev(dk=1))]

    def own_features(a):
        mine = xall[a].reshape(TOK, FEAT)
        part[a] = dot_nn(mine, win[k]) if a == 0 else dot_nt(mine, wout[k])

    def chip_sum(a, half):
        theirs = xsib[a, pl.ds(half * (NX // 2), NX // 2)].reshape(128, FEAT)
        more = dot_nn(theirs, win_sib[...]) if a == 0 else dot_nt(theirs, wout_sib[...])
        return part[a, rows(half, 128), :] + more

    def send_over_z(a):
        zsend[a] = chip_sum(a, 1 - zl).astype(BF16)
        copies = []
        for d in RING8 + (0,):
            block = rows((y + d) % NY, CHUNK)
            copies.append(send(zsend.at[a, block], zrecv.at[a, block], dev(dzl=1)))
        return copies

    def send_over_y(a, zcopy):
        copies = []
        for d, copy in zip(RING8, zcopy):
            copy.wait_recv()
            block = rows((y + d) % NY, CHUNK)
            ysend[a, d] = (own[a, block, :] + zrecv[a, block, :].astype(F32)).astype(BF16)
            copies.append(send(ysend.at[a, d], yrecv.at[a, d], dev(dy=d)))
        return copies

    a3 = pass_to_core(0)
    for copy in local:
        copy.wait()
    own_features(0)
    s_win.wait_recv()
    for copy in a3:
        copy.wait_recv()
    z0 = send_over_z(0)
    a3 = pass_to_core(1)
    own[0] = chip_sum(0, zl)
    own_features(1)
    s_wout.wait_recv()
    for copy in a3:
        copy.wait_recv()
    z1 = send_over_z(1)
    y0 = send_over_y(0, z0)
    own[1] = chip_sum(1, zl)
    y1 = send_over_y(1, z1)

    def chunk(a, half, d):
        return act.at[a, k, rows(half * NY + (y + d) % NY, CHUNK)]

    def finish_sum(a, zlast, ycopy):
        zlast.wait_recv()
        block = rows(y, CHUNK)
        total = own[a, block, :] + zrecv[a, block, :].astype(F32)
        for d, copy in zip(RING8, ycopy):
            copy.wait_recv()
            total = total + yrecv[a, d].astype(F32)
        slot = rows(zl * NY + y, CHUNK)
        if a == 0:
            hidden, slope = gelu_and_slope(total)
            slope_ref[...] = slope
            act[a, k, slot, :] = hidden.astype(BF16)
        else:
            act[a, k, slot, :] = (total * slope_ref[...]).astype(BF16)
        ref = chunk(a, zl, 0)
        near = {d: send(ref, ref, dev(dy=d)) for d in (2, -2, 1, -1)}
        over_z = {0: send(ref, ref, dev(dzl=1))}
        return near, over_z, []

    def pass_near(a):
        near, over_z, _ = ccopy[a]
        near[2].wait_recv()
        near[-2].wait_recv()
        left, right, far = chunk(a, zl, -2), chunk(a, zl, 2), chunk(a, zl, -2 * turn)
        last = []
        for ref, d in ((far, 2 * turn), (left, 1), (right, -1)):
            last.append([send(ref, ref, dev(dy=d, dzl=dzl)) for dzl in (1, 0)])
        for d in (-2, 2, -1, 1):
            if abs(d) == 1:
                near[-d].wait_recv()
            ref = chunk(a, zl, d)
            over_z[d] = send(ref, ref, dev(dzl=1))
        return last

    def pass_last(a, last):
        for half, copies in ((zl, [c[1] for c in last]), (1 - zl, list(ccopy[a][1].values()) + [c[0] for c in last])):
            for copy in copies:
                copy.wait_recv()
            ref = act.at[a, k, rows(half, 128)]
            ccopy[a][2].append(send(ref, ref, dev(dk=1)))

    def model_width(a, half):
        return dot_nn(act[a, half], wout[half]) if a == 0 else dot_nt(act[a, half], win[half])

    def send_over_x(a):
        oacc[...] = model_width(a, k)
        for copy in ccopy[a][2]:
            copy.wait_recv()
        total = oacc[...] + model_width(a, 1 - k)
        total = total.reshape(NX, NZH, CHUNK, FEAT)
        oown[a] = total
        opart[a] = total.astype(BF16)
        return [
            [
                send(opart.at[a, (x + e) % NX, (zh + d) % NZH], xrecv.at[a, d, e], dev(dx=e))
                for e in RING4
            ]
            for d in RING4 + (0,)
        ]

    def sum_over_x(a, d, copies):
        total = oown[a, x, (zh + d) % NZH]
        for e, copy in zip(RING4, copies):
            copy.wait_recv()
            total = total + xrecv[a, d, e].astype(F32)
        return total

    def send_over_zh(a, xcopy):
        copies = []
        for d, group in zip(RING4, xcopy):
            osend[a, d] = sum_over_x(a, d, group)
            copies.append(send(osend.at[a, d], orecv.at[a, d], dev(dzh=d)))
        return copies

    turn = 1 - 2 * (y % 2)
    ccopy = [finish_sum(0, z0[7], y0)]
    ccopy.append(finish_sum(1, z1[7], y1))
    last0 = pass_near(0)
    last1 = pass_near(1)
    pass_last(0, last0)
    x0 = send_over_x(0)
    pass_last(1, last1)
    x1 = send_over_x(1)
    o0 = send_over_zh(0, x0)
    for h in range(2):
        gwout_ref[pl.ds(h * HALF, HALF), :] = dot_tn(act[0, h], xall[1].reshape(TOK, FEAT)).astype(BF16)
    o1 = send_over_zh(1, x1)
    for h in range(2):
        gwin_ref[:, pl.ds(h * HALF, HALF)] = dot_tn(xall[0].reshape(TOK, FEAT), act[1, h]).astype(BF16)
    late = o0 + o1
    for copy in sent:
        if all(copy is not other for other in late):
            copy.wait_send()
    for a, (ref, xcopy, copies) in enumerate(((out_ref, x0, o0), (gin_ref, x1, o1))):
        total = sum_over_x(a, 0, xcopy[3])
        for d, copy in zip(RING4, copies):
            copy.wait_recv()
            total = total + orecv[a, d]
        ref[...] = total.astype(BF16)

    for copy in late:
        copy.wait_send()


N_SENDS = 2 + 2 * (3 + 12 + 1 + 8 + 7 + 4 + 6 + 5 + 2 + 12 + 3)


def place(*refs):
    parts = []
    n, sem = (len(refs) - 1) // 2, refs[-1]
    for i in range(n):
        parts.append(pltpu.make_async_copy(refs[i], refs[n + i], sem.at[i]))
        parts[-1].start()
    for part in parts:
        part.wait()


def on_device(inputs, w_in, w_out, out_grad):
    shapes = (
        jax.ShapeDtypeStruct((CHUNK, FEAT), BF16),
        jax.ShapeDtypeStruct((CHUNK, FEAT), BF16),
        jax.ShapeDtypeStruct((FEAT, HID), BF16),
        jax.ShapeDtypeStruct((HID, FEAT), BF16),
    )
    vmem = pl.BlockSpec(memory_space=pltpu.VMEM)
    hbm = pl.BlockSpec(memory_space=pl.ANY)
    flops = 6 * 2 * TOK * FEAT * HID
    results = pl.pallas_call(
        kernel,
        out_shape=shapes,
        in_specs=[hbm, hbm, hbm, hbm],
        out_specs=(vmem, vmem, vmem, vmem),
        scratch_shapes=[
            pltpu.VMEM((2, FEAT, HALF), BF16),
            pltpu.VMEM((2, HALF, FEAT), BF16),
            pltpu.VMEM((FEAT, HALF), BF16),
            pltpu.VMEM((HALF, FEAT), BF16),
            pltpu.VMEM((2, NX, NZH, CHUNK, FEAT), BF16),
            pltpu.VMEM((2, NX, NZH, CHUNK, FEAT), BF16),
            pltpu.VMEM((2, TOK, HALF), F32),
            pltpu.VMEM((2, 128, HALF), BF16),
            pltpu.VMEM((2, 128, HALF), BF16),
            pltpu.VMEM((2, 128, HALF), F32),
            pltpu.VMEM((2, NY, CHUNK, HALF), BF16),
            pltpu.VMEM((2, NY, CHUNK, HALF), BF16),
            pltpu.VMEM((CHUNK, HALF), F32),
            pltpu.VMEM((2, 2, TOK, HALF), BF16),
            pltpu.VMEM((2, NX, NZH, CHUNK, FEAT), BF16),
            pltpu.VMEM((2, NZH, NX, CHUNK, FEAT), BF16),
            pltpu.VMEM((TOK, FEAT), F32),
            pltpu.VMEM((2, NX, NZH, CHUNK, FEAT), F32),
            pltpu.VMEM((2, NZH, CHUNK, FEAT), F32),
            pltpu.VMEM((2, NZH, CHUNK, FEAT), F32),
            pltpu.SemaphoreType.DMA((N_SENDS,)),
            pltpu.SemaphoreType.DMA((N_SENDS,)),
            pltpu.SemaphoreType.DMA((6,)),
        ],
        compiler_params=pltpu.CompilerParams(
            collective_id=0, has_side_effects=True, vmem_limit_bytes=40 * 1024 * 1024
        ),
        cost_estimate=pl.CostEstimate(flops=flops, bytes_accessed=4 * 2 * FEAT * HID, transcendentals=CHUNK * HALF),
        name="mlp_block",
    )(*(pltpu.with_memory_space_constraint(v, pltpu.HBM) for v in (inputs, out_grad, w_in, w_out)))
    return pl.pallas_call(
        place,
        out_shape=shapes,
        in_specs=[hbm] * 4,
        out_specs=[hbm] * 4,
        scratch_shapes=[pltpu.SemaphoreType.DMA((4,))],
        compiler_params=pltpu.CompilerParams(vmem_limit_bytes=4 * 1024 * 1024),
        name="place_results",
    )(*results)


def solution(mesh):
    return jax.shard_map(
        on_device,
        mesh=mesh,
        in_specs=(P("col", "row"), P("row", "col"), P("col", "row"), P("col", "row")),
        out_specs=(P("col", "row"), P("col", "row"), P("row", "col"), P("col", "row")),
        check_vma=False,
    )
```

```python
import jax
import jax.numpy as jnp
from jax import lax
from jax.experimental import pallas as pl
from jax.experimental.pallas import tpu as pltpu
from jax.sharding import PartitionSpec as P

MESH = pl.DeviceIdType.MESH
BF16, F32 = jnp.bfloat16, jnp.float32
NY, NZL, NK, NX, NZH = 8, 2, 2, 4, 4
TOK, FEAT, HID, HALF = 256, 384, 1536, 768
CHUNK = 16
RING8 = (4, 3, 5, 2, 6, 1, 7)
RING4 = (2, 1, 3)

gelu_coef = 0.7978845608028654


def gelu_and_slope(value):
    inner = gelu_coef * (value + 0.044715 * value * value * value)
    tanh_val = jnp.tanh(inner)
    gelu = 0.5 * value * (1.0 + tanh_val)
    slope = 0.5 * (1.0 + tanh_val) + 0.5 * value * (1.0 - tanh_val * tanh_val) * gelu_coef * (
        1.0 + 3.0 * 0.044715 * value * value
    )
    return gelu, slope


def dot_nn(a, b):
    return lax.dot_general(a, b, (((1,), (0,)), ((), ())), preferred_element_type=F32)


def dot_nt(a, b):
    return lax.dot_general(a, b, (((1,), (1,)), ((), ())), preferred_element_type=F32)


def dot_tn(a, b):
    return lax.dot_general(a, b, (((0,), (0,)), ((), ())), preferred_element_type=F32)


def rows(index, size):
    return pl.ds(pl.multiple_of(index * size, size), size)


def kernel(
    inp_hbm, og_hbm, win_hbm, wout_hbm,
    out_ref, gin_ref, gwin_ref, gwout_ref,
    win, wout, win_sib, wout_sib, xall, xsib,
    part, zsend, zrecv, own, ysend, yrecv, slope_ref, act,
    opart, xrecv, oacc, oown, osend, orecv,
    ssem, rsem, lsem,
):
    r, col = lax.axis_index("row"), lax.axis_index("col")
    y, zl, k = r // 4, (r // 2) % 2, r % 2
    x, zh = col // 4, col % 4

    def dev(dy=0, dzl=0, dk=0, dx=0, dzh=0):
        row = (((y + dy) % NY) * 2 + (zl + dzl) % 2) * 2 + (k + dk) % 2
        return (row, ((x + dx) % NX) * 4 + (zh + dzh) % NZH)

    partners = (
        [dev(dzh=2), dev(dy=4), dev(dy=3), dev(dy=-3)]
        + [dev(dzh=d) for d in (1, 3)]
        + [dev(dy=d, dzl=1) for d in (2, -2)]
        + [dev(dy=d) for d in (2, -2)]
        + [dev(dx=d) for d in RING4]
        + [dev(dy=d, dzl=1) for d in (1, -1)]
        + [dev(dy=d) for d in (1, -1)]
        + [dev(dzl=1), dev(dk=1)]
    )
    barrier = pltpu.get_barrier_semaphore()
    for partner in partners:
        pl.semaphore_signal(barrier, inc=1, device_id=partner, device_id_type=MESH)
    count = [0]
    sent = []

    def send(src, dst, to):
        i = count[0]
        count[0] += 1
        copy = pltpu.make_async_remote_copy(
            src_ref=src, dst_ref=dst, send_sem=ssem.at[i], recv_sem=rsem.at[i],
            device_id=to, device_id_type=MESH,
        )
        copy.start()
        sent.append(copy)
        return copy

    own_in = [
        pltpu.make_async_copy(inp_hbm, xall.at[0, x, zh], lsem.at[4]),
        pltpu.make_async_copy(og_hbm, xall.at[1, x, zh], lsem.at[5]),
    ]
    for copy in own_in:
        copy.start()
    local = []
    for h in range(2):
        cols = pl.ds(h * HALF, HALF)
        local.append(pltpu.make_async_copy(win_hbm.at[:, cols], win.at[h], lsem.at[2 * h]))
        local.append(pltpu.make_async_copy(wout_hbm.at[cols, :], wout.at[h], lsem.at[2 * h + 1]))
    for copy in local:
        copy.start()

    pl.semaphore_wait(barrier, len(partners))

    shards = (inp_hbm, og_hbm)

    def send_shard(a, over):
        return [send(shards[a], xall.at[a, x, zh], dev(**{over: d})) for d in RING4]

    by_zh = [send_shard(0, "dzh"), send_shard(1, "dzh")]
    by_x = [[send_shard(0, "dx")]]
    other = rows(1 - k, HALF)
    by_x.append([send_shard(1, "dx")])
    s_win = send(win_hbm.at[:, other], win_sib, dev(dk=1))
    s_wout = send(wout_hbm.at[other, :], wout_sib, dev(dk=1))
    for a in range(2):
        for d in (1, 3, 2):
            by_zh[a][RING4.index(d)].wait_recv()
            ref = xall.at[a, x, (zh - d) % NZH]
            by_x[a].append([send(ref, ref, dev(dx=e)) for e in RING4])

    def pass_to_core(a):
        own_in[a].wait()
        for group in by_x[a]:
            for copy in group:
                copy.wait_recv()
        return [send(xall.at[a], xsib.at[a], dev(dk=1))]

    def own_features(a):
        mine = xall[a].reshape(TOK, FEAT)
        part[a] = dot_nn(mine, win[k]) if a == 0 else dot_nt(mine, wout[k])

    def chip_sum(a, half):
        theirs = xsib[a, pl.ds(half * (NX // 2), NX // 2)].reshape(128, FEAT)
        more = dot_nn(theirs, win_sib[...]) if a == 0 else dot_nt(theirs, wout_sib[...])
        return part[a, rows(half, 128), :] + more

    def send_over_z(a):
        zsend[a] = chip_sum(a, 1 - zl).astype(BF16)
        copies = []
        for d in RING8 + (0,):
            block = rows((y + d) % NY, CHUNK)
            copies.append(send(zsend.at[a, block], zrecv.at[a, block], dev(dzl=1)))
        return copies

    def send_over_y(a, zcopy):
        copies = []
        for d, copy in zip(RING8, zcopy):
            copy.wait_recv()
            block = rows((y + d) % NY, CHUNK)
            ysend[a, d] = (own[a, block, :] + zrecv[a, block, :].astype(F32)).astype(BF16)
            copies.append(send(ysend.at[a, d], yrecv.at[a, d], dev(dy=d)))
        return copies

    a3 = pass_to_core(0)
    for copy in local:
        copy.wait()
    own_features(0)
    s_win.wait_recv()
    for copy in a3:
        copy.wait_recv()
    z0 = send_over_z(0)
    a3 = pass_to_core(1)
    own[0] = chip_sum(0, zl)
    own_features(1)
    s_wout.wait_recv()
    for copy in a3:
        copy.wait_recv()
    z1 = send_over_z(1)
    own[1] = chip_sum(1, zl)
    y0 = send_over_y(0, z0)
    y1 = send_over_y(1, z1)

    def chunk(a, half, d):
        return act.at[a, k, rows(half * NY + (y + d) % NY, CHUNK)]

    def finish_sum(a, zlast, ycopy):
        zlast.wait_recv()
        block = rows(y, CHUNK)
        total = own[a, block, :] + zrecv[a, block, :].astype(F32)
        for d, copy in zip(RING8, ycopy):
            copy.wait_recv()
            total = total + yrecv[a, d].astype(F32)
        slot = rows(zl * NY + y, CHUNK)
        if a == 0:
            hidden, slope = gelu_and_slope(total)
            slope_ref[...] = slope
            act[a, k, slot, :] = hidden.astype(BF16)
        else:
            act[a, k, slot, :] = (total * slope_ref[...]).astype(BF16)
        ref = chunk(a, zl, 0)
        near = {d: send(ref, ref, dev(dy=d)) for d in (2, -2, 1, -1)}
        over_z = {0: send(ref, ref, dev(dzl=1))}
        return near, over_z, []

    def pass_near(a):
        near, over_z, _ = ccopy[a]
        near[2].wait_recv()
        near[-2].wait_recv()
        left, right, far = chunk(a, zl, -2), chunk(a, zl, 2), chunk(a, zl, -2 * turn)
        last = []
        for ref, d in ((far, 2 * turn), (left, 1), (right, -1)):
            last.append([send(ref, ref, dev(dy=d, dzl=dzl)) for dzl in (1, 0)])
        for d in (-2, 2, -1, 1):
            if abs(d) == 1:
                near[-d].wait_recv()
            ref = chunk(a, zl, d)
            over_z[d] = send(ref, ref, dev(dzl=1))
        return last

    def pass_last(a, last):
        for half, copies in ((zl, [c[1] for c in last]), (1 - zl, list(ccopy[a][1].values()) + [c[0] for c in last])):
            for copy in copies:
                copy.wait_recv()
            ref = act.at[a, k, rows(half, 128)]
            ccopy[a][2].append(send(ref, ref, dev(dk=1)))

    def model_width(a, half):
        return dot_nn(act[a, half], wout[half]) if a == 0 else dot_nt(act[a, half], win[half])

    def send_over_x(a):
        oacc[...] = model_width(a, k)
        for copy in ccopy[a][2]:
            copy.wait_recv()
        total = oacc[...] + model_width(a, 1 - k)
        total = total.reshape(NX, NZH, CHUNK, FEAT)
        oown[a] = total
        opart[a] = total.astype(BF16)
        return [
            [
                send(opart.at[a, (x + e) % NX, (zh + d) % NZH], xrecv.at[a, d, e], dev(dx=e))
                for e in RING4
            ]
            for d in RING4 + (0,)
        ]

    def sum_over_x(a, d, copies):
        total = oown[a, x, (zh + d) % NZH]
        for e, copy in zip(RING4, copies):
            copy.wait_recv()
            total = total + xrecv[a, d, e].astype(F32)
        return total

    def send_over_zh(a, xcopy):
        copies = []
        for d, group in zip(RING4, xcopy):
            osend[a, d] = sum_over_x(a, d, group).astype(BF16)
            copies.append(send(osend.at[a, d], orecv.at[a, d], dev(dzh=d)))
        return copies

    turn = 1 - 2 * (y % 2)
    ccopy = [finish_sum(0, z0[7], y0)]
    ccopy.append(finish_sum(1, z1[7], y1))
    last0 = pass_near(0)
    last1 = pass_near(1)
    pass_last(0, last0)
    x0 = send_over_x(0)
    pass_last(1, last1)
    x1 = send_over_x(1)
    o0 = send_over_zh(0, x0)
    for h in range(2):
        gwout_ref[pl.ds(h * HALF, HALF), :] = dot_tn(act[0, h], xall[1].reshape(TOK, FEAT)).astype(BF16)
    o1 = send_over_zh(1, x1)
    for h in range(2):
        gwin_ref[:, pl.ds(h * HALF, HALF)] = dot_tn(xall[0].reshape(TOK, FEAT), act[1, h]).astype(BF16)
    late = o0 + o1
    for copy in sent:
        if all(copy is not other for other in late):
            copy.wait_send()
    for a, (ref, xcopy, copies) in enumerate(((out_ref, x0, o0), (gin_ref, x1, o1))):
        total = sum_over_x(a, 0, xcopy[3])
        for d, copy in zip(RING4, copies):
            copy.wait_recv()
            total = total + orecv[a, d].astype(F32)
        ref[...] = total.astype(BF16)

    for copy in late:
        copy.wait_send()


N_SENDS = 2 + 2 * (3 + 12 + 1 + 8 + 7 + 4 + 6 + 5 + 2 + 12 + 3)


def place(*refs):
    parts = []
    n, sem = (len(refs) - 1) // 2, refs[-1]
    for i in range(n):
        parts.append(pltpu.make_async_copy(refs[i], refs[n + i], sem.at[i]))
        parts[-1].start()
    for part in parts:
        part.wait()


def on_device(inputs, w_in, w_out, out_grad):
    shapes = (
        jax.ShapeDtypeStruct((CHUNK, FEAT), BF16),
        jax.ShapeDtypeStruct((CHUNK, FEAT), BF16),
        jax.ShapeDtypeStruct((FEAT, HID), BF16),
        jax.ShapeDtypeStruct((HID, FEAT), BF16),
    )
    vmem = pl.BlockSpec(memory_space=pltpu.VMEM)
    hbm = pl.BlockSpec(memory_space=pl.ANY)
    flops = 6 * 2 * TOK * FEAT * HID
    results = pl.pallas_call(
        kernel,
        out_shape=shapes,
        in_specs=[hbm, hbm, hbm, hbm],
        out_specs=(vmem, vmem, vmem, vmem),
        scratch_shapes=[
            pltpu.VMEM((2, FEAT, HALF), BF16),
            pltpu.VMEM((2, HALF, FEAT), BF16),
            pltpu.VMEM((FEAT, HALF), BF16),
            pltpu.VMEM((HALF, FEAT), BF16),
            pltpu.VMEM((2, NX, NZH, CHUNK, FEAT), BF16),
            pltpu.VMEM((2, NX, NZH, CHUNK, FEAT), BF16),
            pltpu.VMEM((2, TOK, HALF), F32),
            pltpu.VMEM((2, 128, HALF), BF16),
            pltpu.VMEM((2, 128, HALF), BF16),
            pltpu.VMEM((2, 128, HALF), F32),
            pltpu.VMEM((2, NY, CHUNK, HALF), BF16),
            pltpu.VMEM((2, NY, CHUNK, HALF), BF16),
            pltpu.VMEM((CHUNK, HALF), F32),
            pltpu.VMEM((2, 2, TOK, HALF), BF16),
            pltpu.VMEM((2, NX, NZH, CHUNK, FEAT), BF16),
            pltpu.VMEM((2, NZH, NX, CHUNK, FEAT), BF16),
            pltpu.VMEM((TOK, FEAT), F32),
            pltpu.VMEM((2, NX, NZH, CHUNK, FEAT), F32),
            pltpu.VMEM((2, NZH, CHUNK, FEAT), BF16),
            pltpu.VMEM((2, NZH, CHUNK, FEAT), BF16),
            pltpu.SemaphoreType.DMA((N_SENDS,)),
            pltpu.SemaphoreType.DMA((N_SENDS,)),
            pltpu.SemaphoreType.DMA((6,)),
        ],
        compiler_params=pltpu.CompilerParams(
            collective_id=0, has_side_effects=True, vmem_limit_bytes=40 * 1024 * 1024
        ),
        cost_estimate=pl.CostEstimate(flops=flops, bytes_accessed=4 * 2 * FEAT * HID, transcendentals=CHUNK * HALF),
        name="mlp_block",
    )(*(pltpu.with_memory_space_constraint(v, pltpu.HBM) for v in (inputs, out_grad, w_in, w_out)))
    return pl.pallas_call(
        place,
        out_shape=shapes,
        in_specs=[hbm] * 4,
        out_specs=[hbm] * 4,
        scratch_shapes=[pltpu.SemaphoreType.DMA((4,))],
        compiler_params=pltpu.CompilerParams(vmem_limit_bytes=4 * 1024 * 1024),
        name="place_results",
    )(*results)


def solution(mesh):
    return jax.shard_map(
        on_device,
        mesh=mesh,
        in_specs=(P("col", "row"), P("row", "col"), P("col", "row"), P("col", "row")),
        out_specs=(P("col", "row"), P("col", "row"), P("row", "col"), P("col", "row")),
        check_vma=False,
    )
```
